256 devices in a mesh: dp: 16 (over z, y_hi), mp: 16 (over x, y_lo, core).
Axes of the slice: x: 4, y: 4 (y_hi: 2, y_lo: 2; y = y_hi * 2 + y_lo), z: 8, core: 2. Of those that a mesh axis runs over, the one named last changes fastest.
Arguments:
- grad_parts: bfloat16 [16, 1024, 16384], P('dp', None, 'mp'), may hold values from -24 to 24
- params: bfloat16 [1024, 16384], P('dp', 'mp'), may hold values from -6 to 6
- stale_left: bfloat16 [16, 1024, 1024], P('mp'), may hold values from -1 to 2
- stale_right: bfloat16 [16, 1024, 1024], P('mp'), may hold values from -1 to 2
- step_matrix: int32 [16], replicated, may hold values from 0 to 31, as said below
Outputs:
- new_params: float32 [1024, 16384], P('dp', 'mp')
- left_roots: bfloat16 [16, 1024, 1024], P('mp', 'dp')
- right_roots: bfloat16 [16, 1024, 1024], P('mp', 'dp')
The draws below stay inside these ranges and needn't reach their ends.
Inputs may be any that keep to these rules, and one draw needn't show every extreme that they name: The 16 entries are distinct. Owner o refreshes statistic step_matrix[o]: that of block step_matrix[o] // 2, the left one if the entry is even, the right one if it is odd. A block may have none, one or both of its statistics refreshed.
All inputs are finite; a program needn't handle non-finite values.
Results may differ from the reference program's by a relative error of at most 0.0045.
Values may be sent and summed in bfloat16 or wider, within the bound.
A program may use at most 128 MiB of HBM per device.

```python
import math
import jax
import jax.numpy as jnp
from jax import lax

BLK = 1024
ITERS = 2
NBLK = 16
N_DP = 16
N_MP = 16


MIX = 0.3


def mix_rows(values, key):
    key_one, key_two, key_three = jax.random.split(key, 3)
    mixed = values + MIX * jnp.take(values, jax.random.permutation(key_one, BLK), axis=1)
    mixed = mixed + MIX * jnp.take(values, jax.random.permutation(key_two, BLK), axis=1)
    mixed = mixed + MIX * jnp.take(values, jax.random.permutation(key_three, BLK), axis=1)
    return mixed


def mix_columns(values, key):
    key_one, key_two, key_three = jax.random.split(key, 3)
    shaped = values.reshape(N_DP, BLK, NBLK, BLK)
    mixed = shaped + MIX * jnp.take(shaped, jax.random.permutation(key_one, BLK), axis=3)
    mixed = mixed + MIX * jnp.take(shaped, jax.random.permutation(key_two, BLK), axis=3)
    mixed = mixed + MIX * jnp.take(shaped, jax.random.permutation(key_three, BLK), axis=3)
    return mixed.reshape(N_DP, BLK, NBLK * BLK)


def draw_grad_parts(key, part):
    key = jax.random.fold_in(key, 11)
    key_rows = jax.random.fold_in(key, 0)
    key_cols = jax.random.fold_in(key, 1)
    key_base = jax.random.fold_in(key, 2)
    key_mixrow = jax.random.fold_in(key, 4)
    key_mixcol = jax.random.fold_in(key, 5)
    place_rows = jnp.arange(BLK, dtype=jnp.float32) / (BLK - 1)
    place_cols = (jnp.arange(NBLK * BLK) % BLK).astype(jnp.float32) / (BLK - 1)
    rows_scale = jnp.exp(jax.random.uniform(key_rows, (1, BLK, 1), minval=0.0, maxval=math.log(2.5)))
    cols_scale = jnp.exp(jax.random.uniform(key_cols, (1, 1, NBLK * BLK), minval=0.0, maxval=math.log(2.5)))
    ramp_rows = jnp.sqrt(1.0 + 2.0 * place_rows)
    ramp_cols = jnp.sqrt(1.0 + 2.0 * place_cols)
    base = jnp.clip(jax.random.normal(key_base, (N_DP, BLK, NBLK * BLK)), -4.0, 4.0)
    base = mix_columns(mix_rows(base, key_mixrow), key_mixcol)
    value = 0.45 * base * rows_scale * cols_scale * ramp_rows[None, :, None] * ramp_cols[None, None, :]
    return jnp.clip(value, -24.0, 24.0).astype(jnp.bfloat16)


def assemble_root(key, offdiag):
    diag_vals = jnp.exp(jax.random.uniform(key, (NBLK, BLK), minval=math.log(0.5), maxval=math.log(2.0)))
    eye = jnp.eye(BLK, dtype=jnp.float32)
    value = offdiag * (0.35 / math.sqrt(BLK)) + eye[None] * diag_vals[:, :, None]
    return jnp.clip(value, -1.0, 2.0).astype(jnp.bfloat16)


def draw_stale_left(key, part):
    key = jax.random.fold_in(key, 12)
    key_diag, key_off = jax.random.split(key)
    offdiag = jnp.clip(jax.random.normal(key_off, (NBLK, BLK, BLK)), -6.0, 6.0)
    return assemble_root(key_diag, offdiag)


def draw_stale_right(key, part):
    key = jax.random.fold_in(key, 13)
    key_diag, key_off = jax.random.split(key)
    offdiag = jnp.clip(jax.random.normal(key_off, (NBLK, BLK, BLK)), -6.0, 6.0)
    return assemble_root(key_diag, offdiag)


def draw_step_matrix(key, part):
    key = jax.random.fold_in(key, 14)
    key_pick, key_order = jax.random.split(key)
    middle = jax.random.permutation(key_pick, 2 * NBLK - 2)[:N_MP - 2] + 1
    ends = jnp.array([0, 2 * NBLK - 1], dtype=jnp.int32)
    values = jnp.concatenate([ends, middle.astype(jnp.int32)])
    return jax.random.permutation(key_order, values).astype(jnp.int32)


def levels(key, extent, cuts, smallest, high):
    level, own = 1.0, jax.random.fold_in(key, 6)
    for axis_at, blocks in cuts:
        steps = jnp.exp(jax.random.uniform(jax.random.fold_in(own, axis_at), (blocks,), jnp.float32, smallest / len(cuts), high / len(cuts)))
        level = level * jnp.repeat(steps, extent[axis_at] // blocks).reshape([-1 if axis == axis_at else 1 for axis in range(len(extent))])
    return level


def gaussian(own_key, shape, deviation, limit, cuts=(), kind=jnp.bfloat16):
    result = jax.random.normal(own_key, shape, jnp.float32) * deviation
    if len(cuts) > 0:
        result = levels(own_key, shape, cuts, -0.22, 0.18) * result
    return jnp.clip(result, min=-limit, max=limit).astype(kind)


def setup_inputs(seed: int = 0) -> dict:
    key_of = jax.random.split(jax.random.key(seed), 6)
    return {
        "grad_parts": draw_grad_parts(jax.random.fold_in(key_of[5], 71), 0),
        "params": gaussian(key_of[1], (BLK, NBLK * BLK), 1.0, 6.0, ((0, 16), (1, 16))),
        "stale_left": draw_stale_left(jax.random.fold_in(key_of[5], 71), 0),
        "stale_right": draw_stale_right(jax.random.fold_in(key_of[5], 71), 0),
        "step_matrix": draw_step_matrix(jax.random.fold_in(key_of[5], 71), 0),
    }


EPS = 1e-6
DAMP = 0.05
STEP_SIZE = 0.5
HIGH = lax.Precision.HIGHEST


def reference(grad_parts, params, stale_left, stale_right, step_matrix):
    eye = jnp.eye(BLK, dtype=jnp.float32)

    def root_of(chosen):
        block_id = (chosen // 2).astype(jnp.int32)
        side_id = chosen % 2
        blockg = lax.dynamic_slice_in_dim(grad_parts, block_id * BLK, BLK, 2).astype(jnp.float32)
        blockg = jnp.where(side_id == 0, blockg, jnp.swapaxes(blockg, 1, 2))
        statistic = jnp.einsum("pik,pjk->ij", blockg, blockg, precision=HIGH)
        scale = 2.0 * jnp.trace(statistic) / BLK + EPS
        current = statistic / scale + DAMP * eye
        root = eye
        for step in range(ITERS):
            factor = (5.0 * eye - current) * 0.25
            root = jnp.dot(root, factor, precision=HIGH)
            power = jnp.dot(factor, factor, precision=HIGH)
            power = jnp.dot(power, factor, precision=HIGH)
            power = jnp.dot(power, factor, precision=HIGH)
            current = jnp.dot(power, 5.0 * eye - 4.0 * factor, precision=HIGH)
        return root.astype(jnp.bfloat16)

    new_root = lax.map(root_of, step_matrix)
    blocks = jnp.arange(NBLK, dtype=jnp.int32)

    def refresh(offset, stale):
        hits = step_matrix[None, :] == (2 * blocks + offset)[:, None]
        fresh = jnp.einsum("ko,oij->kij", hits.astype(jnp.float32), new_root.astype(jnp.float32), precision=HIGH)
        found = jnp.any(hits, axis=1)[:, None, None]
        return jnp.where(found, fresh.astype(jnp.bfloat16), stale)

    left_roots = refresh(0, stale_left)
    right_roots = refresh(1, stale_right)

    def update_block(block_id):
        blockg = lax.dynamic_slice_in_dim(grad_parts, block_id * BLK, BLK, 2).astype(jnp.float32)
        projected = jnp.einsum("pij,jl->pil", blockg, stale_right[block_id].astype(jnp.float32), precision=HIGH).astype(jnp.bfloat16)
        summed = jnp.sum(projected.astype(jnp.float32), axis=0)
        return jnp.dot(stale_left[block_id].astype(jnp.float32), summed, precision=HIGH) / N_DP

    update = lax.map(update_block, blocks)
    update = jnp.transpose(update, (1, 0, 2)).reshape(BLK, NBLK * BLK)
    new_params = params.astype(jnp.float32) - STEP_SIZE * update
    return (new_params, left_roots, right_roots)
```

```python
import functools

import jax
import jax.numpy as jnp
from jax import lax
from jax.experimental import pallas as pl
from jax.experimental.pallas import tpu as pltpu
from jax.sharding import PartitionSpec as P

EPS = 1e-06
DAMP = 0.05
STEP_SIZE = 0.5
RING = 8
PLANES = 2
TILE = 128
PACKED = 5 * TILE
DISTANCES = (4, 3, -3, 2, -2, 1, -1, 0)
SLOT = {distance: slot for slot, distance in enumerate(DISTANCES)}
F32 = jnp.float32
BF16 = jnp.bfloat16
UP, DOWN = 0, 1


def remote(src, dst, sems, at, device):
    return pltpu.make_async_remote_copy(
        src_ref=src,
        dst_ref=dst,
        send_sem=sems[0].at[at],
        recv_sem=sems[1].at[at],
        device_id=device,
        device_id_type=pl.DeviceIdType.MESH,
    )


def tile_at(index):
    return pl.ds(pl.multiple_of(index * TILE, TILE), TILE)


def kernel(
    g_hbm, left_hbm, right_hbm, update_out, roots_out,
    both, left, right, mine, other, lg, lg_tmp,
    mz_send, mz_recv, oz_send, oz_recv, uy_send, uy_recv, uz_send, uz_recv,
    swap_send, swap_recv, packed, full, root_rows, root_recv,
    load_sem, mz_ss, mz_rs, oz_ss, oz_rs, uy_ss, uy_rs, uz_ss, uz_rs, ag_ss, ag_rs, pair_ss, pair_rs,
):
    width = left.shape[0]
    half = TILE // 2
    group, column = lax.axis_index("dp"), lax.axis_index("mp")
    z, plane = group // PLANES, group % PLANES
    other_plane = 1 - plane

    def ring(distance):
        return lax.rem(z + distance + RING, RING)

    up = (ring(1) * PLANES + plane, column)
    down = (ring(-1) * PLANES + plane, column)
    pair = (z * PLANES + other_plane, column)
    toward = (up, down)

    loads = [
        pltpu.make_async_copy(g_hbm.at[0], both.at[plane, :, pl.ds(0, width)], load_sem.at[0]),
        pltpu.make_async_copy(
            g_hbm.at[0, :, pl.ds(0, width // 2)], both.at[plane, :, pl.ds(width, width // 2)], load_sem.at[1]
        ),
        pltpu.make_async_copy(left_hbm.at[0], left, load_sem.at[2]),
        pltpu.make_async_copy(right_hbm.at[0], right, load_sem.at[3]),
    ]
    for load in loads:
        load.start()
    barrier = pltpu.get_barrier_semaphore()
    for neighbour in (up, down, pair):
        pl.semaphore_signal(barrier, inc=1, device_id=neighbour, device_id_type=pl.DeviceIdType.MESH)
    loads[0].wait()
    loads[1].wait()

    for row in range(width // TILE):
        turned = both[plane, row * TILE : (row + 1) * TILE, 0:width].T
        both[other_plane, :, row * TILE : (row + 1) * TILE] = turned
        if row < width // TILE // 2:
            both[other_plane, :, width + row * TILE : width + (row + 1) * TILE] = turned

    def statistic(slot):
        chunk = ring(DISTANCES[slot])
        rows = tile_at(chunk)
        columns = pl.ds(pl.multiple_of(chunk * TILE, TILE), PACKED)
        other[slot] = jnp.dot(both[1, rows, 0:width], both[0, :, columns], preferred_element_type=F32)
        mine[slot] = jnp.dot(both[0, rows, 0:width], both[1, :, columns], preferred_element_type=F32)

    streams = {
        "mz": (mine, mz_send, mz_recv, (mz_ss, mz_rs)),
        "oz": (other, oz_send, oz_recv, (oz_ss, oz_rs)),
        "uz": (lg, uz_send, uz_recv, (uz_ss, uz_rs)),
    }

    def ring_copy(name, step, way):
        own, send, recv, sems = streams[name]
        rows = own.shape[1]
        if step == 0:
            part = pl.ds(way * (rows // 2), rows // 2)
            return remote(send.at[0, 0, part], recv.at[0, 0, part], sems, (0, way), toward[way])
        return remote(send.at[step, way], recv.at[step, way], sems, (step, way), toward[way])

    def ring_step(name, step):
        own, send, recv, sems = streams[name]
        rows = own.shape[1]
        if step == 0:
            send[0, 0] = own[0].astype(BF16)
            for way in (UP, DOWN):
                ring_copy(name, 0, way).start()
            return
        for way in (UP, DOWN):
            slot = SLOT[(4 - step) * (1 if way == UP else -1)]
            ring_copy(name, step - 1, way).wait_recv()
            if step == 1:
                lo, hi = way * (rows // 2), (way + 1) * (rows // 2)
                rest_lo, rest_hi = (1 - way) * (rows // 2), (2 - way) * (rows // 2)
                send[1, way, lo:hi] = (own[slot, lo:hi] + recv[0, 0, lo:hi].astype(F32)).astype(BF16)
                send[1, way, rest_lo:rest_hi] = own[slot, rest_lo:rest_hi].astype(BF16)
            else:
                send[step, way] = (own[slot] + recv[step - 1, way].astype(F32)).astype(BF16)
            ring_copy(name, step, way).start()

    def ring_total(name):
        own, send, recv, sems = streams[name]
        ring_copy(name, 3, UP).wait_recv()
        ring_copy(name, 3, DOWN).wait_recv()
        return own[7] + recv[3, UP].astype(F32) + recv[3, DOWN].astype(F32)

    def update_copy(slot):
        return remote(uy_send.at[slot], uy_recv.at[slot], (uy_ss, uy_rs), slot, pair)

    def update_part(slot):
        rows = tile_at(ring(DISTANCES[slot]))
        lg_tmp[...] = jnp.dot(left[rows, :], both[plane, :, 0:width], preferred_element_type=F32)
        uy_send[slot] = lg_tmp[pl.ds(pl.multiple_of(other_plane * half, half), half), :].astype(BF16)
        update_copy(slot).start()
        lg[slot] = lg_tmp[pl.ds(pl.multiple_of(plane * half, half), half), :]

    def update_join(slot):
        update_copy(slot).wait_recv()
        lg[slot] = lg[slot] + uy_recv[slot].astype(F32)

    statistic(0)
    pl.semaphore_wait(barrier, 3)
    ring_step("oz", 0)
    ring_step("mz", 0)
    statistic(1)
    statistic(2)
    ring_step("oz", 1)
    ring_step("mz", 1)
    statistic(3)
    statistic(4)
    loads[2].wait()
    for slot in range(4):
        update_part(slot)
    ring_step("oz", 2)
    ring_step("mz", 2)
    statistic(5)
    statistic(6)
    statistic(7)
    for slot in range(4, 8):
        update_part(slot)
    ring_step("oz", 3)
    ring_step("mz", 3)
    swap = remote(swap_send, swap_recv, (pair_ss, pair_rs), 0, pair)
    swap_send[...] = ring_total("oz").astype(BF16)
    swap.start()
    mine[7] = ring_total("mz")
    update_join(0)
    ring_step("uz", 0)
    for slot in (1, 2):
        update_join(slot)
    ring_step("uz", 1)
    swap.wait_recv()
    packed[z] = (mine[7] + swap_recv[...].astype(F32)).astype(BF16)

    def gather_copy(step, way, part):
        chunk = ring(-step if way == UP else step)
        piece = packed.at[chunk, pl.ds(part * half, half)]
        return remote(piece, piece, (ag_ss, ag_rs), (step, way, part), toward[way])

    def gather_wait(step, way, part):
        chunk = ring(-step - 1 if way == UP else step + 1)
        piece = packed.at[chunk, pl.ds(part * half, half)]
        remote(piece, piece, (ag_ss, ag_rs), (step, way, part), toward[way]).wait_recv()

    def unpack(distance):
        chunk = ring(distance)
        for offset in range(5):
            block = packed[chunk, :, offset * TILE : (offset + 1) * TILE]
            place = lax.rem(chunk + offset, RING)
            full[tile_at(chunk), tile_at(place)] = block
            if offset in (1, 2, 3):
                full[tile_at(place), tile_at(chunk)] = block.T

    def gathers(step):
        return [(way, part) for part in (0, 1) for way in (UP, DOWN) if step < 3 or part == way]

    for way, part in gathers(0):
        gather_copy(0, way, part).start()
    unpack(0)
    for step in (1, 2, 3):
        for part in (0, 1):
            for way in (UP, DOWN):
                gather_wait(step - 1, way, part)
                if (way, part) in gathers(step):
                    gather_copy(step, way, part).start()
        unpack(-step)
        unpack(step)
    for slot in (3, 4):
        update_join(slot)
    ring_step("uz", 2)
    for way, part in gathers(3):
        gather_wait(3, way, part)
    unpack(4)

    eye = lax.broadcasted_iota(jnp.int32, (TILE, TILE), 0) == lax.broadcasted_iota(jnp.int32, (TILE, TILE), 1)
    diagonal = jnp.zeros((TILE, TILE), F32)
    for tile in range(width // TILE):
        at = slice(tile * TILE, (tile + 1) * TILE)
        diagonal = diagonal + jnp.where(eye, full[at, at].astype(F32), 0.0)
    trace = jnp.sum(jnp.sum(diagonal, axis=0, keepdims=True), axis=1, keepdims=True)
    mean = trace / width
    inverse = 0.25 / (2.0 * mean + EPS)
    for tile in range(width // TILE):
        at = slice(tile * TILE, (tile + 1) * TILE)
        full[at, at] = (full[at, at].astype(F32) - jnp.where(eye, mean, 0.0)).astype(BF16)
    c = (5.0 - DAMP) * 0.25 - mean * inverse
    c2 = c * c
    c3 = c2 * c
    c4 = c2 * c2
    coefficients = [
        1.25 * c - 1.25 * c4 * c + c3 * c3,
        -(1.25 - 6.25 * c4 + 6.0 * c4 * c),
        -12.5 * c3 + 15.0 * c4,
        12.5 * c2 - 20.0 * c3,
        -6.25 * c + 15.0 * c2,
        1.25 - 6.0 * c,
    ]
    own_rows = full[tile_at(z), :].astype(F32) * inverse
    value = own_rows
    for power in (5, 4, 3, 2, 1):
        value = (
            jnp.dot(value.astype(BF16), full[...], preferred_element_type=F32) * inverse
            + coefficients[power] * own_rows
        )
        if power == 3:
            for slot in (5, 6):
                update_join(slot)
            ring_step("uz", 3)
    on_diagonal = (
        lax.broadcasted_iota(jnp.int32, (TILE, width), 0) + z * TILE
        == lax.broadcasted_iota(jnp.int32, (TILE, width), 1)
    )
    root_rows[...] = (value + jnp.where(on_diagonal, coefficients[0], 0.0)).astype(BF16)
    own_half = pl.ds(pl.multiple_of(plane * half, half), half)
    other_half = pl.ds(pl.multiple_of(other_plane * half, half), half)
    send_root = remote(root_rows.at[other_half], root_recv, (pair_ss, pair_rs), 1, pair)
    send_root.start()
    roots_out[plane] = root_rows[own_half, :]

    update_join(7)
    loads[3].wait()
    update_out[...] = jnp.dot(
        ring_total("uz").astype(BF16), right[...], preferred_element_type=F32
    ) / (RING * PLANES)
    send_root.wait_recv()
    roots_out[other_plane] = root_recv[...]

    for name in streams:
        for step in range(4):
            for way in (UP, DOWN):
                ring_copy(name, step, way).wait_send()
    for slot in range(8):
        update_copy(slot).wait_send()
    for step in range(4):
        for way, part in gathers(step):
            gather_copy(step, way, part).wait_send()
    swap.wait_send()
    send_root.wait_send()


def fused(grad_parts, stale_left, stale_right):
    width = grad_parts.shape[1]
    half = TILE // 2
    hbm = pl.BlockSpec(memory_space=pl.ANY)
    vmem = pl.BlockSpec(memory_space=pltpu.VMEM)
    dma = pltpu.SemaphoreType.DMA
    return pl.pallas_call(
        kernel,
        out_shape=(
            jax.ShapeDtypeStruct((half, width), F32),
            jax.ShapeDtypeStruct((PLANES, half, width), BF16),
        ),
        in_specs=[hbm] * 3,
        out_specs=(vmem, vmem),
        scratch_shapes=[
            pltpu.VMEM((2, width, width + width // 2), BF16),
            pltpu.VMEM((width, width), BF16),
            pltpu.VMEM((width, width), BF16),
            pltpu.VMEM((RING, TILE, PACKED), F32),
            pltpu.VMEM((RING, TILE, PACKED), F32),
            pltpu.VMEM((RING, half, width), F32),
            pltpu.VMEM((TILE, width), F32),
            pltpu.VMEM((4, 2, TILE, PACKED), BF16),
            pltpu.VMEM((4, 2, TILE, PACKED), BF16),
            pltpu.VMEM((4, 2, TILE, PACKED), BF16),
            pltpu.VMEM((4, 2, TILE, PACKED), BF16),
            pltpu.VMEM((RING, half, width), BF16),
            pltpu.VMEM((RING, half, width), BF16),
            pltpu.VMEM((4, 2, half, width), BF16),
            pltpu.VMEM((4, 2, half, width), BF16),
            pltpu.VMEM((TILE, PACKED), BF16),
            pltpu.VMEM((TILE, PACKED), BF16),
            pltpu.VMEM((RING, TILE, PACKED), BF16),
            pltpu.VMEM((width, width), BF16),
            pltpu.VMEM((TILE, width), BF16),
            pltpu.VMEM((half, width), BF16),
            dma((4,)),
            dma((4, 2)), dma((4, 2)), dma((4, 2)), dma((4, 2)),
            dma((RING,)), dma((RING,)),
            dma((4, 2)), dma((4, 2)),
            dma((4, 2, 2)), dma((4, 2, 2)),
            dma((2,)), dma((2,)),
        ],
        compiler_params=pltpu.CompilerParams(
            collective_id=0, has_side_effects=True, vmem_limit_bytes=52 << 20
        ),
        name="shampoo",
    )(grad_parts, stale_left, stale_right)


def per_device(grad_parts, params, stale_left, stale_right, step_matrix):
    rows = params.shape[0]
    row_at = lax.axis_index("dp") * rows
    owner = lax.axis_index("mp")
    update, roots = fused(grad_parts, stale_left, stale_right)

    def refreshed(side, stale):
        hit = jnp.any(step_matrix == 2 * owner + side)
        stale_rows = lax.dynamic_slice_in_dim(stale[0], row_at, rows, 0)
        return jnp.where(hit, roots[side], stale_rows)[None]

    new_params = params.astype(F32) - STEP_SIZE * update
    return (new_params, refreshed(0, stale_left), refreshed(1, stale_right))


def solution(mesh):
    return jax.shard_map(
        per_device,
        mesh=mesh,
        in_specs=(
            P("dp", None, "mp"),
            P("dp", "mp"),
            P("mp", None, None),
            P("mp", None, None),
            P(),
        ),
        out_specs=(P("dp", "mp"), P("mp", "dp", None), P("mp", "dp", None)),
        check_vma=False,
    )
```

```python
import jax
import jax.numpy as jnp
from jax import lax
from jax.experimental import pallas as pl
from jax.experimental.pallas import tpu as pltpu
from jax.sharding import PartitionSpec as P

EPS = 1e-06
DAMP = 0.05
STEP_SIZE = 0.5
RING = 8
PLANES = 2
TILE = 128
PACKED = 4 * TILE
RING_FIRST = 3 * TILE
PLANE_ROWS = PACKED - RING_FIRST + TILE // 2
DISTANCES = (4, 3, -3, 2, -2, 1, -1, 0)
SLOT = {distance: slot for slot, distance in enumerate(DISTANCES)}
F32 = jnp.float32
BF16 = jnp.bfloat16
UP, DOWN = 0, 1


SCHEDULE = (
    ("others", 0),
    ("ring_step", "oz", 0),
    ("mines", 0),
    ("ring_step", "mz", 0),
    ("statistic", 1),
    ("statistic", 2),
    ("join", 0),
    ("ring_step", "my", 0),
    ("statistic", 3),
    ("statistic", 4),
    ("ring_step", "oz", 1),
    ("ring_step", "mz", 1),
    ("statistic", 5),
    ("statistic", 6),
    ("statistic", 7),
    ("join", 1),
    ("join", 2),
    ("ring_step", "my", 1),
    ("ring_step", "oz", 2),
    ("ring_step", "mz", 2),
    ("load_wait", 2),
    ("update_part", 0),
    ("update_part", 1),
    ("update_part", 2),
    ("update_part", 3),
    ("join", 3),
    ("join", 4),
    ("ring_step", "my", 2),
    ("ring_step", "oz", 3),
    ("ring_step", "mz", 3),
    ("join", 5),
    ("join", 6),
    ("ring_step", "my", 3),
    ("update_join", 0),
    ("ring_step", "uz", 0),
    ("swap_start",),
    ("update_part", 4),
    ("update_part", 5),
    ("update_part", 6),
    ("update_part", 7),
    ("join", 7),
    ("total_y",),
    ("gather_step", 0, 0),
    ("total_z",),
    ("update_join", 1),
    ("update_join", 2),
    ("swap_done",),
    ("gather_step", 1, 0),
    ("ring_step", "uz", 1),
    ("unpack", 0, 0),
    ("unpack", 1, 0),
    ("gather_step", 0, 1),
    ("unpack", 0, 1, -1),
    ("gather_step", 1, 1),
    ("unpack", 1, 1, -1),
    ("gather_step", 0, 2),
    ("unpack", 0, 2, -2),
    ("gather_step", 1, 2),
    ("unpack", 1, 2, -2),
    ("gather_step", 0, 3),
    ("unpack", 0, 3, -3),
    ("gather_step", 1, 3),
    ("unpack", 1, 3, -3),
    ("update_join", 3),
    ("update_join", 4),
    ("ring_step", "uz", 2),
    ("gather_done", 0),
    ("unpack", 0, 4),
    ("unpack_far", 0, 1, 2, 3),
    ("gather_done", 1),
    ("unpack", 1, 4),
    ("center",),
    ("newton", 5, 4, 3),
    ("update_join", 5),
    ("update_join", 6),
    ("ring_step", "uz", 3),
    ("newton", 2, 1),
    ("root_send",),
    ("update_join", 7),
    ("load_wait", 3),
    ("load_wait", 4),
    ("update_final",),
    ("roots_final",),
)


def remote(src, dst, sems, at, device):
    return pltpu.make_async_remote_copy(
        src_ref=src,
        dst_ref=dst,
        send_sem=sems[0].at[at],
        recv_sem=sems[1].at[at],
        device_id=device,
        device_id_type=pl.DeviceIdType.MESH,
    )


def tile_at(index):
    return pl.ds(pl.multiple_of(index * TILE, TILE), TILE)


def kernel(
    step_hbm, g_hbm, left_hbm, right_hbm, update_out, left_out, right_out,
    both, left, right, mz, oz, my, lg, lg_tmp,
    mz_send, mz_recv, oz_send, oz_recv, my_send, my_recv, uz_send, uz_recv,
    sy_send, sy_recv, uy_send, uy_recv,
    swap_send, swap_recv, packed_z, packed_y, full, root_rows, root_recv, roots,
    step_ref, load_sem, mz_ss, mz_rs, oz_ss, oz_rs, my_ss, my_rs, uz_ss, uz_rs,
    sy_ss, sy_rs, uy_ss, uy_rs, ag_ss, ag_rs, pair_ss, pair_rs,
):
    width = left.shape[0]
    half = TILE // 2
    group, column = lax.axis_index("dp"), lax.axis_index("mp")
    z, plane = group // PLANES, group % PLANES
    other_plane = 1 - plane

    def ring(distance):
        return lax.rem(z + distance + RING, RING)

    up = (ring(1) * PLANES + plane, column)
    down = (ring(-1) * PLANES + plane, column)
    pair = (z * PLANES + other_plane, column)
    toward = (up, down)
    own_half = pl.ds(pl.multiple_of(plane * half, half), half)
    other_half = pl.ds(pl.multiple_of(other_plane * half, half), half)

    started, waiting = [], {}

    def start(key, copy):
        copy.start()
        started.append(copy)
        waiting[key] = copy

    def received(key, copy):
        copy.wait_recv()
        del waiting[key]

    barrier = pltpu.get_barrier_semaphore()
    for neighbour in (up, down, pair):
        pl.semaphore_signal(barrier, inc=1, device_id=neighbour, device_id_type=pl.DeviceIdType.MESH)
    loads = [
        pltpu.make_async_copy(g_hbm.at[0], both.at[plane, :, pl.ds(0, width)], load_sem.at[0]),
        pltpu.make_async_copy(
            g_hbm.at[0, :, pl.ds(0, PACKED - TILE)], both.at[plane, :, pl.ds(width, PACKED - TILE)], load_sem.at[1]
        ),
        pltpu.make_async_copy(left_hbm.at[0], left, load_sem.at[2]),
        pltpu.make_async_copy(right_hbm.at[0], right, load_sem.at[3]),
        pltpu.make_async_copy(step_hbm, step_ref, load_sem.at[4]),
    ]
    loads[0].start()
    loads[1].start()
    loads[0].wait()
    loads[1].wait()
    for load in loads[2:]:
        load.start()

    for row in range(width // TILE):
        turned = both[plane, row * TILE : (row + 1) * TILE, 0:width].T
        both[other_plane, :, row * TILE : (row + 1) * TILE] = turned
        if row < PACKED // TILE - 1:
            both[other_plane, :, width + row * TILE : width + (row + 1) * TILE] = turned

    def plane_copy(slot):
        return remote(sy_send.at[slot], sy_recv.at[slot], (sy_ss, sy_rs), slot, pair)

    def product(slot, first, second, whole, pieces):
        chunk = ring(DISTANCES[slot])
        rows = tile_at(chunk)
        columns = pl.ds(pl.multiple_of(chunk * TILE, TILE), PACKED)
        tiles = jnp.dot(both[first, rows, 0:width], both[second, :, columns], preferred_element_type=F32)
        whole[slot] = tiles[:, :RING_FIRST]
        for at in range(RING_FIRST, PACKED, TILE):
            pieces[slot, at - RING_FIRST : at - RING_FIRST + TILE] = tiles[:, at : at + TILE].astype(pieces.dtype)
        upper = chunk // 4
        rows = pl.ds(pl.multiple_of((chunk - 4 * upper) * TILE + upper * half, half), half)
        columns = tile_at(chunk - 4 * upper + 4)
        tile = jnp.dot(both[first, rows, 0:width], both[second, :, columns], preferred_element_type=F32)
        pieces[slot, PLANE_ROWS - half :] = tile.astype(pieces.dtype)

    def others(*slots):
        for slot in slots:
            product(slot, 1, 0, oz, sy_send)
            start(("sy", slot), plane_copy(slot))

    def mines(*slots):
        for slot in slots:
            product(slot, 0, 1, mz, my)

    def statistic(*slots):
        for slot in slots:
            others(slot)
            mines(slot)

    def join(*slots):
        for slot in slots:
            received(("sy", slot), plane_copy(slot))
            my[slot] = my[slot] + sy_recv[slot].astype(F32)

    streams = {
        "mz": (mz, mz_send, mz_recv, (mz_ss, mz_rs)),
        "oz": (oz, oz_send, oz_recv, (oz_ss, oz_rs)),
        "my": (my, my_send, my_recv, (my_ss, my_rs)),
        "uz": (lg, uz_send, uz_recv, (uz_ss, uz_rs)),
    }

    def ring_copy(name, step, way):
        own, send, recv, sems = streams[name]
        rows = own.shape[1]
        if step == 0:
            part = pl.ds(way * (rows // 2), rows // 2)
            return remote(send.at[0, 0, part], recv.at[0, 0, part], sems, (0, way), toward[way])
        return remote(send.at[step, way], recv.at[step, way], sems, (step, way), toward[way])

    def ring_step(name, step):
        own, send, recv, sems = streams[name]
        rows = own.shape[1]
        if step == 0:
            send[0, 0] = own[0].astype(BF16)
            for way in (UP, DOWN):
                start((name, 0, way), ring_copy(name, 0, way))
            return
        for way in (UP, DOWN):
            slot = SLOT[(4 - step) * (1 if way == UP else -1)]
            received((name, step - 1, way), ring_copy(name, step - 1, way))
            if step == 1:
                lo, hi = way * (rows // 2), (way + 1) * (rows // 2)
                rest_lo, rest_hi = (1 - way) * (rows // 2), (2 - way) * (rows // 2)
                send[1, way, lo:hi] = (own[slot, lo:hi] + recv[0, 0, lo:hi].astype(F32)).astype(BF16)
                send[1, way, rest_lo:rest_hi] = own[slot, rest_lo:rest_hi].astype(BF16)
            else:
                send[step, way] = (own[slot] + recv[step - 1, way].astype(F32)).astype(BF16)
            start((name, step, way), ring_copy(name, step, way))

    def ring_total(name):
        own, send, recv, sems = streams[name]
        received((name, 3, UP), ring_copy(name, 3, UP))
        received((name, 3, DOWN), ring_copy(name, 3, DOWN))
        return own[7] + recv[3, UP].astype(F32) + recv[3, DOWN].astype(F32)

    def update_copy(slot):
        return remote(uy_send.at[slot], uy_recv.at[slot], (uy_ss, uy_rs), slot, pair)

    def update_part(*slots):
        for slot in slots:
            rows = tile_at(ring(DISTANCES[slot]))
            lg_tmp[...] = jnp.dot(left[rows, :], both[plane, :, 0:width], preferred_element_type=F32)
            uy_send[slot] = lg_tmp[other_half, :].astype(BF16)
            start(("uy", slot), update_copy(slot))
            lg[slot] = lg_tmp[own_half, :]

    def update_join(*slots):
        for slot in slots:
            received(("uy", slot), update_copy(slot))
            lg[slot] = lg[slot] + uy_recv[slot].astype(F32)

    parts = (packed_y, packed_z)

    def gather_copy(part, step, way):
        piece = parts[part].at[ring(-step if way == UP else step)]
        return remote(piece, piece, (ag_ss, ag_rs), (part, step, way), toward[way])

    def gather_wait(part, step, way):
        piece = parts[part].at[ring(-step - 1 if way == UP else step + 1)]
        received(("ag", part, step, way), remote(piece, piece, (ag_ss, ag_rs), (part, step, way), toward[way]))

    def gather_ways(part, step):
        return (UP, DOWN) if step < 3 else (part,)

    def gather_step(part, step):
        for way in (UP, DOWN):
            if step > 0:
                gather_wait(part, step - 1, way)
            if way in gather_ways(part, step):
                start(("ag", part, step, way), gather_copy(part, step, way))

    def place(rows, columns, block, turned):
        full[rows, columns] = block
        if turned:
            full[columns, rows] = block.T

    def unpack(part, *distances):
        for distance in distances:
            chunk = ring(distance)
            for offset in range(PACKED // TILE):
                at = offset * TILE
                if (at < RING_FIRST) == (part == 1):
                    block = (
                        packed_z[chunk, :, at : at + TILE]
                        if part == 1
                        else packed_y[chunk, at - RING_FIRST : at - RING_FIRST + TILE]
                    )
                    place(tile_at(chunk), tile_at(lax.rem(chunk + offset, RING)), block, offset > 0)

    def unpack_far(*distances):
        for distance in distances:
            lower = lax.rem(ring(distance), 4)
            block = jnp.concatenate(
                [packed_y[lower, PLANE_ROWS - half :], packed_y[lower + 4, PLANE_ROWS - half :]], axis=0
            )
            place(tile_at(lower), tile_at(lower + 4), block, True)

    def load_wait(*which):
        for index in which:
            loads[index].wait()

    def swap_copy():
        return remote(swap_send, swap_recv, (pair_ss, pair_rs), 0, pair)

    def swap_start():
        swap_send[...] = ring_total("oz").astype(BF16)
        start("swap", swap_copy())

    def total_y():
        packed_y[z] = ring_total("my").astype(BF16)

    def total_z():
        mz[7] = ring_total("mz")

    def swap_done():
        received("swap", swap_copy())
        packed_z[z] = (mz[7] + swap_recv[...].astype(F32)).astype(BF16)

    def gather_done(part):
        for way in gather_ways(part, 3):
            gather_wait(part, 3, way)

    state = {}

    def center():
        eye = lax.broadcasted_iota(jnp.int32, (TILE, TILE), 0) == lax.broadcasted_iota(jnp.int32, (TILE, TILE), 1)
        tiles = [slice(at, at + TILE) for at in range(0, width, TILE)]
        diagonal = jnp.zeros((TILE, TILE), F32)
        for at in tiles:
            diagonal = diagonal + jnp.where(eye, full[at, at].astype(F32), 0.0)
        trace = jnp.sum(jnp.sum(diagonal, axis=0, keepdims=True), axis=1, keepdims=True)
        mean = trace / width
        inverse = 0.25 / (2.0 * mean + EPS)
        for at in tiles:
            full[at, at] = (full[at, at].astype(F32) - jnp.where(eye, mean, 0.0)).astype(BF16)
        c = (5.0 - DAMP) * 0.25 - mean * inverse
        c2 = c * c
        c3 = c2 * c
        c4 = c2 * c2
        state["coefficients"] = [
            1.25 * c - 1.25 * c4 * c + c3 * c3,
            -(1.25 - 6.25 * c4 + 6.0 * c4 * c),
            -12.5 * c3 + 15.0 * c4,
            12.5 * c2 - 20.0 * c3,
            -6.25 * c + 15.0 * c2,
            1.25 - 6.0 * c,
        ]
        state["inverse"] = inverse
        state["rows"] = state["value"] = full[tile_at(z), :].astype(F32) * inverse

    def newton(*powers):
        for power in powers:
            state["value"] = (
                jnp.dot(state["value"].astype(BF16), full[...], preferred_element_type=F32) * state["inverse"]
                + state["coefficients"][power] * state["rows"]
            )

    def root_copy():
        return remote(root_rows.at[other_half], root_recv, (pair_ss, pair_rs), 1, pair)

    def root_send():
        on_diagonal = (
            lax.broadcasted_iota(jnp.int32, (TILE, width), 0) + z * TILE
            == lax.broadcasted_iota(jnp.int32, (TILE, width), 1)
        )
        root_rows[...] = (state["value"] + jnp.where(on_diagonal, state["coefficients"][0], 0.0)).astype(BF16)
        start("root", root_copy())
        roots[plane] = root_rows[own_half, :]

    def update_final():
        total = ring_total("uz").astype(BF16)
        update_out[...] = jnp.dot(total, right[...], preferred_element_type=F32) / (RING * PLANES)

    def roots_final():
        received("root", root_copy())
        roots[other_plane] = root_recv[...]
        own_at = pl.ds(pl.multiple_of(group * half, half), half)
        for side, stale, out in ((0, left, left_out), (1, right, right_out)):
            hits = jnp.int32(0)
            for owner in range(step_ref.shape[0]):
                hits = hits + (step_ref[owner] == 2 * column + side).astype(jnp.int32)
            out[0] = jnp.where(jnp.full((half, width), hits) > 0, roots[side], stale[own_at, :])

    pl.semaphore_wait(barrier, 3)
    operations = {
        operation.__name__: operation
        for operation in (
            others, mines, statistic, join, ring_step, load_wait, update_part, update_join, swap_start, swap_done,
            total_y, total_z, gather_step, gather_done, unpack, unpack_far, center, newton, root_send,
            update_final, roots_final,
        )
    }
    for name, *values in SCHEDULE:
        operations[name](*values)

    for copy in started:
        copy.wait_send()


def per_device(grad_parts, params, stale_left, stale_right, step_matrix):
    width = grad_parts.shape[1]
    half = TILE // 2
    hbm = pl.BlockSpec(memory_space=pltpu.HBM)
    vmem = pl.BlockSpec(memory_space=pltpu.VMEM)
    dma = pltpu.SemaphoreType.DMA

    def ring_buffers(rows, columns):
        return [pltpu.VMEM((4, 2, rows, columns), BF16)] * 2

    update, left_roots, right_roots = pl.pallas_call(
        kernel,
        out_shape=(
            jax.ShapeDtypeStruct((half, width), F32),
            jax.ShapeDtypeStruct((1, half, width), BF16),
            jax.ShapeDtypeStruct((1, half, width), BF16),
        ),
        in_specs=[hbm] * 4,
        out_specs=(vmem, vmem, vmem),
        scratch_shapes=[
            pltpu.VMEM((2, width, width + PACKED - TILE), BF16),
            pltpu.VMEM((width, width), BF16),
            pltpu.VMEM((width, width), BF16),
            pltpu.VMEM((RING, TILE, RING_FIRST), F32),
            pltpu.VMEM((RING, TILE, RING_FIRST), F32),
            pltpu.VMEM((RING, PLANE_ROWS, TILE), F32),
            pltpu.VMEM((RING, half, width), F32),
            pltpu.VMEM((TILE, width), F32),
            *ring_buffers(TILE, RING_FIRST),
            *ring_buffers(TILE, RING_FIRST),
            *ring_buffers(PLANE_ROWS, TILE),
            *ring_buffers(half, width),
            pltpu.VMEM((RING, PLANE_ROWS, TILE), BF16),
            pltpu.VMEM((RING, PLANE_ROWS, TILE), BF16),
            pltpu.VMEM((RING, half, width), BF16),
            pltpu.VMEM((RING, half, width), BF16),
            pltpu.VMEM((TILE, RING_FIRST), BF16),
            pltpu.VMEM((TILE, RING_FIRST), BF16),
            pltpu.VMEM((RING, TILE, RING_FIRST), BF16),
            pltpu.VMEM((RING, PLANE_ROWS, TILE), BF16),
            pltpu.VMEM((width, width), BF16),
            pltpu.VMEM((TILE, width), BF16),
            pltpu.VMEM((half, width), BF16),
            pltpu.VMEM((2, half, width), BF16),
            pltpu.SMEM((16,), jnp.int32),
            dma((5,)),
            *[dma((4, 2))] * 8,
            *[dma((RING,))] * 4,
            *[dma((2, 4, 2))] * 2,
            *[dma((2,))] * 2,
        ],
        compiler_params=pltpu.CompilerParams(
            collective_id=0, has_side_effects=True, vmem_limit_bytes=52 << 20
        ),
        name="shampoo",
    )(step_matrix, grad_parts, stale_left, stale_right)
    return params.astype(F32) - STEP_SIZE * update, left_roots, right_roots


def solution(mesh):
    return jax.shard_map(
        per_device,
        mesh=mesh,
        in_specs=(
            P("dp", None, "mp"),
            P("dp", "mp"),
            P("mp", None, None),
            P("mp", None, None),
            P(),
        ),
        out_specs=(P("dp", "mp"), P("mp", "dp", None), P("mp", "dp", None)),
        check_vma=False,
    )
```

```python
import jax
import jax.numpy as jnp
from jax import lax
from jax.experimental import pallas as pl
from jax.experimental.pallas import tpu as pltpu
from jax.sharding import PartitionSpec as P

EPS = 1e-06
DAMP = 0.05
STEP_SIZE = 0.5
RING = 8
PLANES = 2
TILE = 128
PACKED = 4 * TILE
RING_FIRST = 2 * TILE
PLANE_ROWS = PACKED - RING_FIRST + TILE // 2
DISTANCES = (4, 3, -3, 2, -2, 1, -1, 0)
SLOT = {distance: slot for slot, distance in enumerate(DISTANCES)}
F32 = jnp.float32
BF16 = jnp.bfloat16
UP, DOWN = 0, 1


OZ, MZ, MY, UZ = range(4)


def remote(src, dst, sems, at, device):
    return pltpu.make_async_remote_copy(
        src_ref=src,
        dst_ref=dst,
        send_sem=sems[0].at[at],
        recv_sem=sems[1].at[at],
        device_id=device,
        device_id_type=pl.DeviceIdType.MESH,
    )


def tile_at(index):
    return pl.ds(pl.multiple_of(index * TILE, TILE), TILE)


def kernel(
    step_hbm, g_hbm, left_hbm, right_hbm, update_out, roots_out,
    both, left, right, mz, oz, my, lg, lg_tmp,
    mz_send, mz_recv, oz_send, oz_recv, my_send, my_recv, uz_send, uz_recv,
    sy_send, sy_recv, uy_send, uy_recv,
    swap_send, swap_recv, packed_z, packed_y, full, root_rows, root_recv, roots,
    step_ref, load_sem, mz_ss, mz_rs, oz_ss, oz_rs, my_ss, my_rs, uz_ss, uz_rs,
    sy_ss, sy_rs, uy_ss, uy_rs, ag_ss, ag_rs, pair_ss, pair_rs,
):
    width = left.shape[0]
    half = TILE // 2
    group, column = lax.axis_index("dp"), lax.axis_index("mp")
    z, plane = group // PLANES, group % PLANES
    other_plane = 1 - plane

    def ring(distance):
        return lax.rem(z + distance + RING, RING)

    up = (ring(1) * PLANES + plane, column)
    down = (ring(-1) * PLANES + plane, column)
    pair = (z * PLANES + other_plane, column)
    toward = (up, down)
    own_half = pl.ds(pl.multiple_of(plane * half, half), half)
    other_half = pl.ds(pl.multiple_of(other_plane * half, half), half)

    started, waiting = [], {}

    def start(key, copy):
        copy.start()
        started.append(copy)
        waiting[key] = copy

    def received(key, copy):
        copy.wait_recv()
        del waiting[key]

    barrier = pltpu.get_barrier_semaphore()
    for neighbour in (up, down, pair):
        pl.semaphore_signal(barrier, inc=1, device_id=neighbour, device_id_type=pl.DeviceIdType.MESH)
    loads = [
        pltpu.make_async_copy(g_hbm.at[0], both.at[plane, :, pl.ds(0, width)], load_sem.at[0]),
        pltpu.make_async_copy(
            g_hbm.at[0, :, pl.ds(0, PACKED - TILE)], both.at[plane, :, pl.ds(width, PACKED - TILE)], load_sem.at[1]
        ),
        pltpu.make_async_copy(left_hbm.at[0], left, load_sem.at[2]),
        pltpu.make_async_copy(right_hbm.at[0], right, load_sem.at[3]),
        pltpu.make_async_copy(step_hbm, step_ref, load_sem.at[4]),
    ]
    loads[0].start()
    loads[1].start()
    loads[0].wait()
    loads[1].wait()
    for load in loads[2:]:
        load.start()

    for row in range(width // TILE):
        turned = both[plane, row * TILE : (row + 1) * TILE, 0:width].T
        both[other_plane, :, row * TILE : (row + 1) * TILE] = turned
        if row < PACKED // TILE - 1:
            both[other_plane, :, width + row * TILE : width + (row + 1) * TILE] = turned

    def plane_copy(slot):
        return remote(sy_send.at[slot], sy_recv.at[slot], (sy_ss, sy_rs), slot, pair)

    def product(slot, first, second, whole, pieces):
        chunk = ring(DISTANCES[slot])
        rows = tile_at(chunk)
        columns = pl.ds(pl.multiple_of(chunk * TILE, TILE), PACKED)
        tiles = jnp.dot(both[first, rows, 0:width], both[second, :, columns], preferred_element_type=F32)
        whole[slot] = tiles[:, :RING_FIRST]
        for at in range(RING_FIRST, PACKED, TILE):
            pieces[slot, at - RING_FIRST : at - RING_FIRST + TILE] = tiles[:, at : at + TILE].astype(pieces.dtype)
        upper = chunk // 4
        rows = pl.ds(pl.multiple_of((chunk - 4 * upper) * TILE + upper * half, half), half)
        columns = tile_at(chunk - 4 * upper + 4)
        tile = jnp.dot(both[first, rows, 0:width], both[second, :, columns], preferred_element_type=F32)
        pieces[slot, PLANE_ROWS - half :] = tile.astype(pieces.dtype)

    def others(*slots):
        for slot in slots:
            product(slot, 1, 0, oz, sy_send)
            start(("sy", slot), plane_copy(slot))

    def mines(*slots):
        for slot in slots:
            product(slot, 0, 1, mz, my)

    def join(*slots):
        for slot in slots:
            received(("sy", slot), plane_copy(slot))
            my[slot] = my[slot] + sy_recv[slot].astype(F32)

    streams = (
        (oz, oz_send, oz_recv, (oz_ss, oz_rs)),
        (mz, mz_send, mz_recv, (mz_ss, mz_rs)),
        (my, my_send, my_recv, (my_ss, my_rs)),
        (lg, uz_send, uz_recv, (uz_ss, uz_rs)),
    )

    def ring_copy(name, step, way):
        own, send, recv, sems = streams[name]
        rows = own.shape[1]
        if step == 0:
            part = pl.ds(way * (rows // 2), rows // 2)
            return remote(send.at[0, 0, part], recv.at[0, 0, part], sems, (0, way), toward[way])
        return remote(send.at[step, way], recv.at[step, way], sems, (step, way), toward[way])

    def ring_step(name, step):
        own, send, recv, sems = streams[name]
        rows = own.shape[1]
        if step == 0:
            send[0, 0] = own[0].astype(BF16)
            for way in (UP, DOWN):
                start((name, 0, way), ring_copy(name, 0, way))
            return
        for way in (UP, DOWN):
            slot = SLOT[(4 - step) * (1 if way == UP else -1)]
            received((name, step - 1, way), ring_copy(name, step - 1, way))
            if step == 1:
                lo, hi = way * (rows // 2), (way + 1) * (rows // 2)
                rest_lo, rest_hi = (1 - way) * (rows // 2), (2 - way) * (rows // 2)
                send[1, way, lo:hi] = (own[slot, lo:hi] + recv[0, 0, lo:hi].astype(F32)).astype(BF16)
                send[1, way, rest_lo:rest_hi] = own[slot, rest_lo:rest_hi].astype(BF16)
            else:
                send[step, way] = (own[slot] + recv[step - 1, way].astype(F32)).astype(BF16)
            start((name, step, way), ring_copy(name, step, way))

    def ring_total(name):
        own, send, recv, sems = streams[name]
        received((name, 3, UP), ring_copy(name, 3, UP))
        received((name, 3, DOWN), ring_copy(name, 3, DOWN))
        return own[7] + recv[3, UP].astype(F32) + recv[3, DOWN].astype(F32)

    def update_copy(slot):
        return remote(uy_send.at[slot], uy_recv.at[slot], (uy_ss, uy_rs), slot, pair)

    def update_make(*slots):
        for slot in slots:
            rows = tile_at(ring(DISTANCES[slot]))
            lg_tmp[...] = jnp.dot(left[rows, :], both[plane, :, 0:width], preferred_element_type=F32)
            uy_send[slot] = lg_tmp[other_half, :].astype(BF16)
            lg[slot] = lg_tmp[own_half, :]

    def update_go(*slots):
        for slot in slots:
            start(("uy", slot), update_copy(slot))

    def update_join(*slots):
        for slot in slots:
            received(("uy", slot), update_copy(slot))
            lg[slot] = lg[slot] + uy_recv[slot].astype(F32)

    parts = (packed_y, packed_z)

    def gather_copy(part, step, way):
        piece = parts[part].at[ring(-step if way == UP else step)]
        return remote(piece, piece, (ag_ss, ag_rs), (part, step, way), toward[way])

    def gather_wait(part, step, way):
        piece = parts[part].at[ring(-step - 1 if way == UP else step + 1)]
        received(("ag", part, step, way), remote(piece, piece, (ag_ss, ag_rs), (part, step, way), toward[way]))

    def gather_ways(part, step):
        return (UP, DOWN) if step < 3 else (part,)

    def gather_step(part, step):
        for way in (UP, DOWN):
            if step > 0:
                gather_wait(part, step - 1, way)
            if way in gather_ways(part, step):
                start(("ag", part, step, way), gather_copy(part, step, way))

    eye = lax.broadcasted_iota(jnp.int32, (TILE, TILE), 0) == lax.broadcasted_iota(jnp.int32, (TILE, TILE), 1)
    state = {"diagonal": jnp.zeros((TILE, TILE), F32)}

    def place(rows, columns, block, turned):
        full[rows, columns] = block
        if turned:
            full[columns, rows] = block.T

    def unpack(part, *distances):
        for distance in distances:
            chunk = ring(distance)
            for offset in range(PACKED // TILE):
                at = offset * TILE
                if (at < RING_FIRST) == (part == 1):
                    block = (
                        packed_z[chunk, :, at : at + TILE]
                        if part == 1
                        else packed_y[chunk, at - RING_FIRST : at - RING_FIRST + TILE]
                    )
                    place(tile_at(chunk), tile_at(lax.rem(chunk + offset, RING)), block, offset > 0)
                    if offset == 0:
                        state["diagonal"] = state["diagonal"] + jnp.where(eye, block.astype(F32), 0.0)

    def unpack_far(*distances):
        for distance in distances:
            lower = lax.rem(ring(distance), 4)
            block = jnp.concatenate(
                [packed_y[lower, PLANE_ROWS - half :], packed_y[lower + 4, PLANE_ROWS - half :]], axis=0
            )
            place(tile_at(lower), tile_at(lower + 4), block, True)

    def load_wait(*which):
        for index in which:
            loads[index].wait()

    def swap_copy():
        return remote(swap_send, swap_recv, (pair_ss, pair_rs), 0, pair)

    def swap_start():
        swap_send[...] = ring_total(OZ).astype(BF16)
        start("swap", swap_copy())

    def total_y():
        packed_y[z] = ring_total(MY).astype(BF16)

    def total_z():
        mz[7] = ring_total(MZ)

    def swap_done():
        received("swap", swap_copy())
        packed_z[z] = (mz[7] + swap_recv[...].astype(F32)).astype(BF16)

    def gather_done(part):
        for way in gather_ways(part, 3):
            gather_wait(part, 3, way)

    on_diagonal = (
        lax.broadcasted_iota(jnp.int32, (TILE, width), 0) + z * TILE
        == lax.broadcasted_iota(jnp.int32, (TILE, width), 1)
    )

    def center():
        trace = jnp.sum(jnp.sum(state["diagonal"], axis=0, keepdims=True), axis=1, keepdims=True)
        mean = trace / width
        inverse = 0.25 / (2.0 * mean + EPS)
        c = (5.0 - DAMP) * 0.25 - mean * inverse
        c2 = c * c
        c3 = c2 * c
        c4 = c2 * c2
        state["coefficients"] = [
            1.25 * c - 1.25 * c4 * c + c3 * c3,
            -(1.25 - 6.25 * c4 + 6.0 * c4 * c),
            -12.5 * c3 + 15.0 * c4,
            12.5 * c2 - 20.0 * c3,
            -6.25 * c + 15.0 * c2,
            1.25 - 6.0 * c,
        ]
        state["inverse"] = inverse
        state["shift"] = mean * inverse
        rows = full[tile_at(z), :].astype(F32)
        state["rows"] = state["value"] = (rows - jnp.where(on_diagonal, mean, 0.0)) * inverse

    def newton(*powers):
        for power in powers:
            value = state["value"].astype(BF16)
            state["value"] = (
                jnp.dot(value, full[...], preferred_element_type=F32) * state["inverse"]
                - value.astype(F32) * state["shift"]
                + state["coefficients"][power] * state["rows"]
            )

    def root_copy():
        return remote(root_rows.at[other_half], root_recv, (pair_ss, pair_rs), 1, pair)

    def root_send():
        root_rows[...] = (state["value"] + jnp.where(on_diagonal, state["coefficients"][0], 0.0)).astype(BF16)
        start("root", root_copy())
        roots[plane] = root_rows[own_half, :]

    def update_final():
        total = ring_total(UZ).astype(BF16)
        update_out[...] = jnp.dot(total, right[...], preferred_element_type=F32) / (RING * PLANES)

    def roots_final():
        received("root", root_copy())
        roots[other_plane] = root_recv[...]
        own_at = pl.ds(pl.multiple_of(group * half, half), half)
        for side, stale in ((0, left), (1, right)):
            hits = jnp.int32(0)
            for owner in range(step_ref.shape[0]):
                hits = hits + (step_ref[owner] == 2 * column + side).astype(jnp.int32)
            roots_out[side] = jnp.where(jnp.full((half, width), hits) > 0, roots[side], stale[own_at, :])

    pl.semaphore_wait(barrier, 3)
    others(0)
    ring_step(OZ, 0)
    mines(0)
    ring_step(MZ, 0)
    others(1)
    mines(1)
    others(2)
    mines(2)
    join(0)
    ring_step(MY, 0)
    others(3)
    mines(3)
    others(4)
    mines(4)
    ring_step(OZ, 1)
    ring_step(MZ, 1)
    others(5)
    mines(5)
    others(6)
    mines(6)
    others(7)
    mines(7)
    load_wait(2)
    update_make(0)
    update_make(1)
    update_make(2)
    join(1, 2)
    ring_step(MY, 1)
    ring_step(OZ, 2)
    ring_step(MZ, 2)
    update_make(3)
    update_make(4)
    update_make(5)
    join(3, 4)
    ring_step(MY, 2)
    join(5, 6)
    update_go(0)
    ring_step(OZ, 3)
    ring_step(MZ, 3)
    update_make(6)
    update_make(7)
    ring_step(MY, 3)
    swap_start()
    update_go(1)
    update_go(2)
    update_go(3)
    update_go(4)
    update_go(5)
    update_go(6)
    update_go(7)
    join(7)
    total_y()
    gather_step(0, 0)
    total_z()
    swap_done()
    gather_step(1, 0)
    update_join(0)
    ring_step(UZ, 0)
    unpack(0, 0)
    unpack(1, 0)
    gather_step(0, 1)
    unpack(0, 1, -1)
    gather_step(1, 1)
    unpack(1, 1, -1)
    gather_step(0, 2)
    unpack(0, 2, -2)
    gather_step(1, 2)
    update_join(1, 2)
    ring_step(UZ, 1)
    unpack(1, 2, -2)
    gather_step(0, 3)
    unpack(0, 3, -3)
    gather_step(1, 3)
    unpack(1, 3, -3)
    update_join(3, 4)
    ring_step(UZ, 2)
    gather_done(0)
    unpack(0, 4)
    unpack_far(0, 1, 2, 3)
    gather_done(1)
    unpack(1, 4)
    center()
    newton(5, 4, 3)
    update_join(5, 6)
    ring_step(UZ, 3)
    newton(2, 1)
    root_send()
    load_wait(4)
    update_join(7)
    load_wait(3)
    update_final()
    roots_final()

    for copy in started:
        copy.wait_send()


def per_device(grad_parts, params, stale_left, stale_right, step_matrix):
    width = grad_parts.shape[1]
    half = TILE // 2
    hbm = pl.BlockSpec(memory_space=pltpu.HBM)
    vmem = pl.BlockSpec(memory_space=pltpu.VMEM)
    dma = pltpu.SemaphoreType.DMA

    def ring_buffers(rows, columns):
        return [pltpu.VMEM((4, 2, rows, columns), BF16)] * 2

    update, both_roots = pl.pallas_call(
        kernel,
        out_shape=(
            jax.ShapeDtypeStruct((half, width), F32),
            jax.ShapeDtypeStruct((PLANES, half, width), BF16),
        ),
        in_specs=[hbm] * 4,
        out_specs=(vmem, vmem),
        scratch_shapes=[
            pltpu.VMEM((2, width, width + PACKED - TILE), BF16),
            pltpu.VMEM((width, width), BF16),
            pltpu.VMEM((width, width), BF16),
            pltpu.VMEM((RING, TILE, RING_FIRST), F32),
            pltpu.VMEM((RING, TILE, RING_FIRST), F32),
            pltpu.VMEM((RING, PLANE_ROWS, TILE), F32),
            pltpu.VMEM((RING, half, width), F32),
            pltpu.VMEM((TILE, width), F32),
            *ring_buffers(TILE, RING_FIRST),
            *ring_buffers(TILE, RING_FIRST),
            *ring_buffers(PLANE_ROWS, TILE),
            *ring_buffers(half, width),
            pltpu.VMEM((RING, PLANE_ROWS, TILE), BF16),
            pltpu.VMEM((RING, PLANE_ROWS, TILE), BF16),
            pltpu.VMEM((RING, half, width), BF16),
            pltpu.VMEM((RING, half, width), BF16),
            pltpu.VMEM((TILE, RING_FIRST), BF16),
            pltpu.VMEM((TILE, RING_FIRST), BF16),
            pltpu.VMEM((RING, TILE, RING_FIRST), BF16),
            pltpu.VMEM((RING, PLANE_ROWS, TILE), BF16),
            pltpu.VMEM((width, width), BF16),
            pltpu.VMEM((TILE, width), BF16),
            pltpu.VMEM((half, width), BF16),
            pltpu.VMEM((2, half, width), BF16),
            pltpu.SMEM((16,), jnp.int32),
            dma((5,)),
            *[dma((4, 2))] * 8,
            *[dma((RING,))] * 4,
            *[dma((2, 4, 2))] * 2,
            *[dma((2,))] * 2,
        ],
        compiler_params=pltpu.CompilerParams(
            collective_id=0, has_side_effects=True, vmem_limit_bytes=52 << 20
        ),
        name="shampoo",
    )(step_matrix, grad_parts, stale_left, stale_right)
    return params.astype(F32) - STEP_SIZE * update, both_roots[:1], both_roots[1:]


def solution(mesh):
    return jax.shard_map(
        per_device,
        mesh=mesh,
        in_specs=(
            P("dp", None, "mp"),
            P("dp", "mp"),
            P("mp", None, None),
            P("mp", None, None),
            P(),
        ),
        out_specs=(P("dp", "mp"), P("mp", "dp", None), P("mp", "dp", None)),
        check_vma=False,
    )
```

```python
import jax
import jax.numpy as jnp
from jax import lax
from jax.experimental import pallas as pl
from jax.experimental.pallas import tpu as pltpu
from jax.sharding import PartitionSpec as P

EPS = 1e-06
DAMP = 0.05
STEP_SIZE = 0.5
RING = 8
PLANES = 2
TILE = 128
PACKED = 4 * TILE
RING_FIRST = 2 * TILE
PLANE_ROWS = PACKED - RING_FIRST + TILE // 2
DISTANCES = (4, 3, -3, 2, -2, 1, -1, 0)
SLOT = {distance: slot for slot, distance in enumerate(DISTANCES)}
F32 = jnp.float32
BF16 = jnp.bfloat16
UP, DOWN = 0, 1


OZ, MZ, MY, UZ = range(4)


def remote(src, dst, sems, at, device):
    return pltpu.make_async_remote_copy(
        src_ref=src,
        dst_ref=dst,
        send_sem=sems[0].at[at],
        recv_sem=sems[1].at[at],
        device_id=device,
        device_id_type=pl.DeviceIdType.MESH,
    )


def tile_at(index):
    return pl.ds(pl.multiple_of(index * TILE, TILE), TILE)


def kernel(
    step_hbm, g_hbm, left_hbm, right_hbm, update_out, roots_out,
    both, left, right, mz, oz, my, lg, lg_tmp,
    mz_send, mz_recv, oz_send, oz_recv, my_send, my_recv, uz_send, uz_recv,
    sy_send, sy_recv, uy_send, uy_recv,
    swap_send, swap_recv, packed_z, packed_y, full, root_rows, root_recv, roots,
    step_ref, load_sem, mz_ss, mz_rs, oz_ss, oz_rs, my_ss, my_rs, uz_ss, uz_rs,
    sy_ss, sy_rs, uy_ss, uy_rs, ag_ss, ag_rs, pair_ss, pair_rs,
):
    width = left.shape[0]
    half = TILE // 2
    group, column = lax.axis_index("dp"), lax.axis_index("mp")
    z, plane = group // PLANES, group % PLANES
    other_plane = 1 - plane

    def ring(distance):
        return lax.rem(z + distance + RING, RING)

    up = (ring(1) * PLANES + plane, column)
    down = (ring(-1) * PLANES + plane, column)
    pair = (z * PLANES + other_plane, column)
    toward = (up, down)
    own_half = pl.ds(pl.multiple_of(plane * half, half), half)
    other_half = pl.ds(pl.multiple_of(other_plane * half, half), half)

    started, waiting = [], {}

    def start(key, copy):
        copy.start()
        started.append(copy)
        waiting[key] = copy

    def received(key, copy):
        copy.wait_recv()
        del waiting[key]

    barrier = pltpu.get_barrier_semaphore()
    for neighbour in (up, down, pair):
        pl.semaphore_signal(barrier, inc=1, device_id=neighbour, device_id_type=pl.DeviceIdType.MESH)
    loads = [
        pltpu.make_async_copy(g_hbm.at[0], both.at[plane, :, pl.ds(0, width)], load_sem.at[0]),
        pltpu.make_async_copy(
            g_hbm.at[0, :, pl.ds(0, PACKED - TILE)], both.at[plane, :, pl.ds(width, PACKED - TILE)], load_sem.at[1]
        ),
        pltpu.make_async_copy(left_hbm.at[0], left, load_sem.at[2]),
        pltpu.make_async_copy(right_hbm.at[0], right, load_sem.at[3]),
        pltpu.make_async_copy(step_hbm, step_ref, load_sem.at[4]),
    ]
    loads[0].start()
    loads[1].start()
    loads[0].wait()
    loads[1].wait()
    for load in loads[2:]:
        load.start()

    for row in range(width // TILE):
        turned = both[plane, row * TILE : (row + 1) * TILE, 0:width].T
        both[other_plane, :, row * TILE : (row + 1) * TILE] = turned
        if row < PACKED // TILE - 1:
            both[other_plane, :, width + row * TILE : width + (row + 1) * TILE] = turned

    def plane_copy(slot):
        return remote(sy_send.at[slot], sy_recv.at[slot], (sy_ss, sy_rs), slot, pair)

    def product(slot, first, second, whole, pieces):
        chunk = ring(DISTANCES[slot])
        rows = tile_at(chunk)
        columns = pl.ds(pl.multiple_of(chunk * TILE, TILE), PACKED)
        tiles = jnp.dot(both[first, rows, 0:width], both[second, :, columns], preferred_element_type=F32)
        whole[slot] = tiles[:, :RING_FIRST]
        for at in range(RING_FIRST, PACKED, TILE):
            pieces[slot, at - RING_FIRST : at - RING_FIRST + TILE] = tiles[:, at : at + TILE].astype(pieces.dtype)
        upper = chunk // 4
        rows = pl.ds(pl.multiple_of((chunk - 4 * upper) * TILE + upper * half, half), half)
        columns = tile_at(chunk - 4 * upper + 4)
        tile = jnp.dot(both[first, rows, 0:width], both[second, :, columns], preferred_element_type=F32)
        pieces[slot, PLANE_ROWS - half :] = tile.astype(pieces.dtype)

    def others(*slots):
        for slot in slots:
            product(slot, 1, 0, oz, sy_send)
            start(("sy", slot), plane_copy(slot))

    def mines(*slots):
        for slot in slots:
            product(slot, 0, 1, mz, my)

    def join(*slots):
        for slot in slots:
            received(("sy", slot), plane_copy(slot))
            my[slot] = my[slot] + sy_recv[slot].astype(F32)

    streams = (
        (oz, oz_send, oz_recv, (oz_ss, oz_rs)),
        (mz, mz_send, mz_recv, (mz_ss, mz_rs)),
        (my, my_send, my_recv, (my_ss, my_rs)),
        (lg, uz_send, uz_recv, (uz_ss, uz_rs)),
    )

    def ring_copy(name, step, way):
        own, send, recv, sems = streams[name]
        rows = own.shape[1]
        if step == 0:
            part = pl.ds(way * (rows // 2), rows // 2)
            return remote(send.at[0, 0, part], recv.at[0, 0, part], sems, (0, way), toward[way])
        return remote(send.at[step, way], recv.at[step, way], sems, (step, way), toward[way])

    def ring_step(name, step):
        own, send, recv, sems = streams[name]
        rows = own.shape[1]
        if step == 0:
            send[0, 0] = own[0].astype(BF16)
            for way in (UP, DOWN):
                start((name, 0, way), ring_copy(name, 0, way))
            return
        for way in (UP, DOWN):
            slot = SLOT[(4 - step) * (1 if way == UP else -1)]
            received((name, step - 1, way), ring_copy(name, step - 1, way))
            if step == 1:
                lo, hi = way * (rows // 2), (way + 1) * (rows // 2)
                rest_lo, rest_hi = (1 - way) * (rows // 2), (2 - way) * (rows // 2)
                send[1, way, lo:hi] = (own[slot, lo:hi] + recv[0, 0, lo:hi].astype(F32)).astype(BF16)
                send[1, way, rest_lo:rest_hi] = own[slot, rest_lo:rest_hi].astype(BF16)
            else:
                send[step, way] = (own[slot] + recv[step - 1, way].astype(F32)).astype(BF16)
            start((name, step, way), ring_copy(name, step, way))

    def ring_total(name):
        own, send, recv, sems = streams[name]
        received((name, 3, UP), ring_copy(name, 3, UP))
        received((name, 3, DOWN), ring_copy(name, 3, DOWN))
        return own[7] + recv[3, UP].astype(F32) + recv[3, DOWN].astype(F32)

    def update_copy(slot):
        return remote(uy_send.at[slot], uy_recv.at[slot], (uy_ss, uy_rs), slot, pair)

    def update_make(*slots):
        for slot in slots:
            rows = tile_at(ring(DISTANCES[slot]))
            lg_tmp[...] = jnp.dot(left[rows, :], both[plane, :, 0:width], preferred_element_type=F32)
            uy_send[slot] = lg_tmp[other_half, :].astype(BF16)
            lg[slot] = lg_tmp[own_half, :]

    def update_go(*slots):
        for slot in slots:
            start(("uy", slot), update_copy(slot))

    def update_join(*slots):
        for slot in slots:
            received(("uy", slot), update_copy(slot))
            lg[slot] = lg[slot] + uy_recv[slot].astype(F32)

    parts = (packed_y, packed_z)

    def gather_copy(part, step, way):
        piece = parts[part].at[ring(-step if way == UP else step)]
        return remote(piece, piece, (ag_ss, ag_rs), (part, step, way), toward[way])

    def gather_wait(part, step, way):
        piece = parts[part].at[ring(-step - 1 if way == UP else step + 1)]
        received(("ag", part, step, way), remote(piece, piece, (ag_ss, ag_rs), (part, step, way), toward[way]))

    def gather_ways(part, step):
        return (UP, DOWN) if step < 3 else (part,)

    def gather_step(part, step):
        for way in (UP, DOWN):
            if step > 0:
                gather_wait(part, step - 1, way)
            if way in gather_ways(part, step):
                start(("ag", part, step, way), gather_copy(part, step, way))

    eye = lax.broadcasted_iota(jnp.int32, (TILE, TILE), 0) == lax.broadcasted_iota(jnp.int32, (TILE, TILE), 1)
    state = {"diagonal": jnp.zeros((TILE, TILE), F32)}

    def place(rows, columns, block, turned):
        full[rows, columns] = block
        if turned:
            full[columns, rows] = block.T

    def unpack(part, *distances):
        for distance in distances:
            chunk = ring(distance)
            for offset in range(PACKED // TILE):
                at = offset * TILE
                if (at < RING_FIRST) == (part == 1):
                    block = (
                        packed_z[chunk, :, at : at + TILE]
                        if part == 1
                        else packed_y[chunk, at - RING_FIRST : at - RING_FIRST + TILE]
                    )
                    place(tile_at(chunk), tile_at(lax.rem(chunk + offset, RING)), block, offset > 0)
                    if offset == 0:
                        state["diagonal"] = state["diagonal"] + jnp.where(eye, block.astype(F32), 0.0)

    def unpack_far(*distances):
        for distance in distances:
            lower = lax.rem(ring(distance), 4)
            block = jnp.concatenate(
                [packed_y[lower, PLANE_ROWS - half :], packed_y[lower + 4, PLANE_ROWS - half :]], axis=0
            )
            place(tile_at(lower), tile_at(lower + 4), block, True)

    def load_wait(*which):
        for index in which:
            loads[index].wait()

    def swap_copy():
        return remote(swap_send, swap_recv, (pair_ss, pair_rs), 0, pair)

    def swap_start():
        swap_send[...] = ring_total(OZ).astype(BF16)
        start("swap", swap_copy())

    def total_y():
        packed_y[z] = ring_total(MY).astype(BF16)

    def total_z():
        mz[7] = ring_total(MZ)

    def swap_done():
        received("swap", swap_copy())
        packed_z[z] = (mz[7] + swap_recv[...].astype(F32)).astype(BF16)

    def gather_done(part):
        for way in gather_ways(part, 3):
            gather_wait(part, 3, way)

    on_diagonal = (
        lax.broadcasted_iota(jnp.int32, (TILE, width), 0) + z * TILE
        == lax.broadcasted_iota(jnp.int32, (TILE, width), 1)
    )

    def center():
        trace = jnp.sum(jnp.sum(state["diagonal"], axis=0, keepdims=True), axis=1, keepdims=True)
        mean = trace / width
        inverse = 0.25 / (2.0 * mean + EPS)
        c = (5.0 - DAMP) * 0.25 - mean * inverse
        c2 = c * c
        c3 = c2 * c
        c4 = c2 * c2
        state["coefficients"] = [
            1.25 * c - 1.25 * c4 * c + c3 * c3,
            -(1.25 - 6.25 * c4 + 6.0 * c4 * c),
            -12.5 * c3 + 15.0 * c4,
            12.5 * c2 - 20.0 * c3,
            -6.25 * c + 15.0 * c2,
            1.25 - 6.0 * c,
        ]
        state["inverse"] = inverse
        state["shift"] = mean * inverse
        rows = full[tile_at(z), :].astype(F32)
        state["rows"] = state["value"] = (rows - jnp.where(on_diagonal, mean, 0.0)) * inverse

    def newton(*powers):
        for power in powers:
            value = state["value"].astype(BF16)
            state["value"] = (
                jnp.dot(value, full[...], preferred_element_type=F32) * state["inverse"]
                - value.astype(F32) * state["shift"]
                + state["coefficients"][power] * state["rows"]
            )

    def root_copy():
        return remote(root_rows.at[other_half], root_recv, (pair_ss, pair_rs), 1, pair)

    def root_send():
        root_rows[...] = (state["value"] + jnp.where(on_diagonal, state["coefficients"][0], 0.0)).astype(BF16)
        start("root", root_copy())
        roots[plane] = root_rows[own_half, :]

    def update_final():
        total = ring_total(UZ).astype(BF16)
        update_out[...] = jnp.dot(total, right[...], preferred_element_type=F32) / (RING * PLANES)

    def roots_final():
        received("root", root_copy())
        roots[other_plane] = root_recv[...]
        own_at = pl.ds(pl.multiple_of(group * half, half), half)
        for side, stale in ((0, left), (1, right)):
            hits = jnp.int32(0)
            for owner in range(step_ref.shape[0]):
                hits = hits + (step_ref[owner] == 2 * column + side).astype(jnp.int32)
            roots_out[side] = jnp.where(jnp.full((half, width), hits) > 0, roots[side], stale[own_at, :])

    pl.semaphore_wait(barrier, 3)
    others(0)
    ring_step(OZ, 0)
    mines(0)
    ring_step(MZ, 0)
    others(1)
    mines(1)
    others(2)
    mines(2)
    join(0)
    ring_step(MY, 0)
    others(3)
    mines(3)
    others(4)
    mines(4)
    ring_step(OZ, 1)
    ring_step(MZ, 1)
    others(5)
    mines(5)
    others(6)
    mines(6)
    others(7)
    mines(7)
    load_wait(2)
    update_make(0)
    update_make(1)
    update_make(2)
    join(1, 2)
    ring_step(MY, 1)
    ring_step(OZ, 2)
    ring_step(MZ, 2)
    update_make(3)
    update_make(4)
    update_make(5)
    join(3, 4)
    ring_step(MY, 2)
    join(5, 6)
    update_go(0)
    ring_step(OZ, 3)
    ring_step(MZ, 3)
    update_make(6)
    update_make(7)
    ring_step(MY, 3)
    swap_start()
    update_go(1)
    update_go(2)
    join(7)
    total_y()
    gather_step(0, 0)
    update_go(3)
    update_join(0)
    ring_step(UZ, 0)
    update_go(4)
    update_go(5)
    update_go(6)
    update_go(7)
    total_z()
    swap_done()
    gather_step(1, 0)
    unpack(0, 0)
    unpack(1, 0)
    gather_step(0, 1)
    unpack(0, 1, -1)
    gather_step(1, 1)
    unpack(1, 1, -1)
    gather_step(0, 2)
    unpack(0, 2, -2)
    gather_step(1, 2)
    update_join(1, 2)
    ring_step(UZ, 1)
    unpack(1, 2, -2)
    gather_step(0, 3)
    unpack(0, 3, -3)
    gather_step(1, 3)
    unpack(1, 3, -3)
    update_join(3, 4)
    ring_step(UZ, 2)
    gather_done(0)
    unpack(0, 4)
    unpack_far(0, 1, 2, 3)
    gather_done(1)
    unpack(1, 4)
    center()
    newton(5, 4, 3)
    update_join(5, 6)
    ring_step(UZ, 3)
    newton(2, 1)
    root_send()
    load_wait(4)
    update_join(7)
    load_wait(3)
    update_final()
    roots_final()

    for copy in started:
        copy.wait_send()


def per_device(grad_parts, params, stale_left, stale_right, step_matrix):
    width = grad_parts.shape[1]
    half = TILE // 2
    hbm = pl.BlockSpec(memory_space=pltpu.HBM)
    vmem = pl.BlockSpec(memory_space=pltpu.VMEM)
    dma = pltpu.SemaphoreType.DMA

    def ring_buffers(rows, columns):
        return [pltpu.VMEM((4, 2, rows, columns), BF16)] * 2

    update, both_roots = pl.pallas_call(
        kernel,
        out_shape=(
            jax.ShapeDtypeStruct((half, width), F32),
            jax.ShapeDtypeStruct((PLANES, half, width), BF16),
        ),
        in_specs=[hbm] * 4,
        out_specs=(vmem, vmem),
        scratch_shapes=[
            pltpu.VMEM((2, width, width + PACKED - TILE), BF16),
            pltpu.VMEM((width, width), BF16),
            pltpu.VMEM((width, width), BF16),
            pltpu.VMEM((RING, TILE, RING_FIRST), F32),
            pltpu.VMEM((RING, TILE, RING_FIRST), F32),
            pltpu.VMEM((RING, PLANE_ROWS, TILE), F32),
            pltpu.VMEM((RING, half, width), F32),
            pltpu.VMEM((TILE, width), F32),
            *ring_buffers(TILE, RING_FIRST),
            *ring_buffers(TILE, RING_FIRST),
            *ring_buffers(PLANE_ROWS, TILE),
            *ring_buffers(half, width),
            pltpu.VMEM((RING, PLANE_ROWS, TILE), BF16),
            pltpu.VMEM((RING, PLANE_ROWS, TILE), BF16),
            pltpu.VMEM((RING, half, width), BF16),
            pltpu.VMEM((RING, half, width), BF16),
            pltpu.VMEM((TILE, RING_FIRST), BF16),
            pltpu.VMEM((TILE, RING_FIRST), BF16),
            pltpu.VMEM((RING, TILE, RING_FIRST), BF16),
            pltpu.VMEM((RING, PLANE_ROWS, TILE), BF16),
            pltpu.VMEM((width, width), BF16),
            pltpu.VMEM((TILE, width), BF16),
            pltpu.VMEM((half, width), BF16),
            pltpu.VMEM((2, half, width), BF16),
            pltpu.SMEM((16,), jnp.int32),
            dma((5,)),
            *[dma((4, 2))] * 8,
            *[dma((RING,))] * 4,
            *[dma((2, 4, 2))] * 2,
            *[dma((2,))] * 2,
        ],
        compiler_params=pltpu.CompilerParams(
            collective_id=0, has_side_effects=True, vmem_limit_bytes=52 << 20
        ),
        name="shampoo",
    )(step_matrix, grad_parts, stale_left, stale_right)
    return params.astype(F32) - STEP_SIZE * update, both_roots[:1], both_roots[1:]


def solution(mesh):
    return jax.shard_map(
        per_device,
        mesh=mesh,
        in_specs=(
            P("dp", None, "mp"),
            P("dp", "mp"),
            P("mp", None, None),
            P("mp", None, None),
            P(),
        ),
        out_specs=(P("dp", "mp"), P("mp", "dp", None), P("mp", "dp", None)),
        check_vma=False,
    )
```
